1024 devices in a mesh: img: 64 (over y, z_hi, core), txt: 16 (over x, z_lo).
Axes of the slice: x: 8, y: 8, z: 8 (z_hi: 4, z_lo: 2; z = z_hi * 2 + z_lo), core: 2. Of those that a mesh axis runs over, the one named last changes fastest.
Arguments:
- images: bfloat16 [16384, 1152], P(('img', 'txt')), may hold values from -6 to 6
- texts: bfloat16 [16384, 1152], P(('txt', 'img')), may hold values from -6 to 6
- log_temp: float32 [1], replicated, may hold values from 1.6 to 2.3
- bias: float32 [1], replicated, may hold values from -7 to -5
Outputs:
- loss: float32 [1], replicated
- grad_images: float32 [16384, 1152], P(('img', 'txt'))
- grad_texts: float32 [16384, 1152], P(('txt', 'img'))
- grad_temp: float32 [1], replicated
- grad_bias: float32 [1], replicated
The draws below stay inside these ranges and needn't reach their ends.
All inputs are finite; a program needn't handle non-finite values.
Results may differ from the reference program's by a relative error of at most 0.0043.
Values may be sent and summed in bfloat16 or wider, within the bound.
A program may use at most 32 MiB of HBM per device.

```python
import math
import jax
import jax.numpy as jnp
from jax import lax

D = 1152
BATCH = 16384


def shared_base(key):
    return jax.random.normal(key, (BATCH, D), jnp.float32)


def draw_images(key, part):
    base = shared_base(key)
    return jnp.clip(base, -6.0, 6.0).astype(jnp.bfloat16)


def draw_texts(key, part):
    base = shared_base(key)
    key = jax.random.fold_in(key, 23)
    key_own, key_mix = jax.random.split(key)
    fresh = jax.random.normal(key_own, (BATCH, D), jnp.float32)
    mixing = jax.random.uniform(key_mix, (BATCH, 1), jnp.float32, 0.4, 0.9)
    paired = mixing * base + jnp.sqrt(1.0 - mixing * mixing) * fresh
    return jnp.clip(paired, -6.0, 6.0).astype(jnp.bfloat16)


def setup_inputs(seed: int = 0) -> dict:
    arg_keys = jax.random.split(jax.random.key(seed), 5)
    images = draw_images(jax.random.fold_in(arg_keys[4], 71), 0)
    texts = draw_texts(jax.random.fold_in(arg_keys[4], 71), 0)
    log_temp = jnp.clip(jax.random.uniform(arg_keys[2], (1,), jnp.float32, 1.6, 2.3), 1.6, 2.3)
    bias = jnp.clip(jax.random.uniform(arg_keys[3], (1,), jnp.float32, -7.0, -5.0), -7.0, -5.0)
    return {"images": images, "texts": texts, "log_temp": log_temp, "bias": bias}


def normalize(embed):
    wide = embed.astype(jnp.float32)
    inverse = lax.rsqrt(lax.optimization_barrier(jnp.sum(wide * wide, axis=-1, keepdims=True)) + 1e-06)
    return (wide * inverse, inverse)

def unnormalize(normed, inverse, grad_normed):
    inner = lax.optimization_barrier(jnp.sum(normed * grad_normed, axis=-1, keepdims=True))
    return inverse * (grad_normed - normed * inner)

def reference(images, texts, log_temp, bias):
    x_norm, inv_x = normalize(images)
    y_norm, inv_y = normalize(texts)
    x_low = x_norm.astype(jnp.bfloat16)
    y_low = y_norm.astype(jnp.bfloat16)
    temp = jnp.exp(log_temp[0])
    shift = bias[0]
    block = math.gcd(BATCH, 512)
    count = BATCH // block
    columns = jnp.arange(BATCH, dtype=jnp.int32)

    def step(carry, index):
        dy_sum, loss_sum, temp_sum, bias_sum = carry
        start = (index * block).astype(jnp.int32)
        rows = lax.dynamic_slice_in_dim(x_low, start, block, 0)
        dots = jnp.dot(rows, y_low.T, preferred_element_type=jnp.float32)
        logits = temp * dots + shift
        row_ids = start + jnp.arange(block, dtype=jnp.int32)
        sign = jnp.where(row_ids[:, None] == columns[None, :], 1.0, -1.0).astype(jnp.float32)
        loss_sum = loss_sum - jnp.sum(jax.nn.log_sigmoid(sign * logits))
        grad_logits = -sign * jax.nn.sigmoid(-sign * logits)
        temp_sum = temp_sum + jnp.sum(grad_logits * dots)
        bias_sum = bias_sum + jnp.sum(grad_logits)
        grad_low = grad_logits.astype(jnp.bfloat16)
        dx_rows = temp * jnp.dot(grad_low, y_low, preferred_element_type=jnp.float32)
        dy_sum = dy_sum + temp * jnp.dot(grad_low.T, rows, preferred_element_type=jnp.float32)
        return ((dy_sum, loss_sum, temp_sum, bias_sum), dx_rows)
    zero = jnp.zeros((), jnp.float32)
    init = (jnp.zeros((BATCH, D), jnp.float32), zero, zero, zero)
    (dy_norm, loss_sum, temp_sum, bias_sum), dx_blocks = lax.scan(step, init, jnp.arange(count, dtype=jnp.int32))
    dx_norm = dx_blocks.reshape(BATCH, D)
    grad_images = unnormalize(x_norm, inv_x, dx_norm)
    grad_texts = unnormalize(y_norm, inv_y, dy_norm)
    loss = (loss_sum / BATCH).reshape(1)
    grad_temp = (temp * temp_sum / BATCH).reshape(1)
    grad_bias = (bias_sum / BATCH).reshape(1)
    return (loss, grad_images, grad_texts, grad_temp, grad_bias)
```

```python
import functools

import jax
import jax.numpy as jnp
from jax import lax
from jax.experimental import pallas as pl
from jax.experimental.pallas import tpu as pltpu
from jax.sharding import PartitionSpec as P

MESH = pl.DeviceIdType.MESH
F32, BF16 = jnp.float32, jnp.bfloat16
NX, NY, NZ = 8, 8, 4
ROWS = 16
FAR_FIRST = (4, 3, 5, 2, 6, 1, 7)


def normalize(embed):
    wide = embed.astype(F32)
    inverse = lax.rsqrt(jnp.sum(wide * wide, axis=-1, keepdims=True) + 1e-06)
    return wide * inverse, inverse


def unnormalize(normed, inverse, grad_normed):
    inner = jnp.sum(normed * grad_normed, axis=-1, keepdims=True)
    return inverse * (grad_normed - normed * inner)


def kernel(
    log_temp_ref, bias_ref, images_ref, texts_ref,
    loss_ref, grad_images_ref, grad_texts_ref, grad_temp_ref, grad_bias_ref,
    XB, YB, GT, DYF, DYB, RY, RZ, RZ1, RY1, TOT, DYN, DXS, RXS, DX0, DXB, RX, RXZ, DXT, PA, PB, PC,
    ss, rs,
):
    img, txt = lax.axis_index("img"), lax.axis_index("txt")
    y, zh, c = img // (NZ * 2), (img // 2) % NZ, img % 2
    x, zl = txt // 2, txt % 2
    width = images_ref.shape[1]

    def device(dx=0, dy=0, dz=0, dl=0, dc=0):
        i = ((((y + dy) % NY) * NZ + (zh + dz) % NZ) * 2) + (c + dc) % 2
        t = ((x + dx) % NX) * 2 + (zl + dl) % 2
        return (i, t)

    names = {}
    sends = {"all": [], 0: [], 1: []}

    def copy_of(name):
        q, src, dst, to = names[name]
        return pltpu.make_async_remote_copy(
            src_ref=src(), dst_ref=dst(), send_sem=ss.at[q], recv_sem=rs.at[q],
            device_id=device(**to), device_id_type=MESH,
        )

    def send(name, src, dst, to, who="all"):
        q = names[name][0] if name in names else len(names)
        names[name] = (q, src, dst, to)
        copy_of(name).start()
        sends[who].append(name)

    def wait(name):
        copy_of(name).wait_recv()

    others = [device(dz=m, dl=a, dc=b) for m in range(NZ) for a in (0, 1) for b in (0, 1) if (m, a, b) != (0, 0, 0)]
    peers = [device(dx=j) for j in range(1, NX)] + [device(dy=j) for j in range(1, NY)] + others
    barrier = pltpu.get_barrier_semaphore()
    for peer in peers:
        pl.semaphore_signal(barrier, inc=1, device_id=peer, device_id_type=MESH)

    x_norm, inv_x = normalize(images_ref[...])
    y_norm, inv_y = normalize(texts_ref[...])
    XB[0, 0, 0] = x_norm.astype(BF16)
    YB[0, 0] = y_norm.astype(BF16)
    pl.semaphore_wait(barrier, len(peers))

    def text_z_own(who):
        for m in (2, 1, 3):
            send(f"tz{m}", lambda m=m: YB.at[0, 0], lambda m=m: YB.at[0, NZ - m], dict(dz=m), who)

    def text_y_own(who):
        for j in FAR_FIRST:
            send(f"ty{j}", lambda j=j: YB.at[0, 0], lambda j=j: YB.at[NY - j, 0], dict(dy=j), who)

    @pl.when(c == 0)
    def _():
        text_z_own(0)

    @pl.when(c == 1)
    def _():
        text_y_own(1)

    send("xl", lambda: XB.at[0, 0, 0], lambda: XB.at[0, 0, 1], dict(dl=1))
    for j in FAR_FIRST:
        send(f"xo{j}", lambda j=j: XB.at[0, 0, 0], lambda j=j: XB.at[0, NX - j, 0], dict(dx=j))

    @pl.when(c == 0)
    def _():
        text_y_own(0)
        for m in (1, 3, 2):
            wait(f"tz{m}")
        for j in FAR_FIRST:
            send(f"tr{j}", lambda j=j: YB.at[0, pl.ds(1, 3)], lambda j=j: YB.at[NY - j, pl.ds(1, 3)], dict(dy=j), 0)

    @pl.when(c == 1)
    def _():
        text_z_own(1)

    wait("xl")
    for j in FAR_FIRST:
        send(f"xp{j}", lambda j=j: XB.at[0, 0, 1], lambda j=j: XB.at[0, NX - j, 1], dict(dx=j))
    send("xs0", lambda: XB.at[0, 0], lambda: XB.at[1, 0], dict(dc=1))

    @pl.when(c == 1)
    def _():
        for j in (1, 7, 2, 6, 3, 5, 4):
            wait(f"ty{j}")
        for m in (2, 1, 3):
            send(f"tw{m}", lambda m=m: YB.at[pl.ds(1, 7), 0], lambda m=m: YB.at[pl.ds(1, 7), NZ - m], dict(dz=m), 1)

    for j in (1, 7, 2, 6, 3, 5, 4):
        wait(f"xo{j}")
        wait(f"xp{j}")
        send(f"xs{NX - j}", lambda j=j: XB.at[0, NX - j], lambda j=j: XB.at[1, NX - j], dict(dc=1))
    for k in range(NX):
        wait(f"xs{k}")

    @pl.when(c == 0)
    def _():
        for j in (1, 7, 2, 6, 3, 5, 4):
            wait(f"ty{j}")
            wait(f"tr{j}")

    @pl.when(c == 1)
    def _():
        for m in (1, 3, 2):
            wait(f"tz{m}")
            wait(f"tw{m}")

    temp = jnp.exp(jnp.full((1, 128), log_temp_ref[0], F32))
    temp_row = jnp.exp(jnp.full((1, 512), log_temp_ref[0], F32))
    shift = bias_ref[0]
    col = lax.broadcasted_iota(jnp.int32, (1, 512), 1)
    col_core = (c + (col >> 8)) & 1
    col_x = (x + ((col >> 5) & 7)) & 7
    col_zl = (zl + ((col >> 4) & 1)) & 1
    col_id = ((y * NZ + zh) * 2 + col_core) * 256 + (col_x * 2 + col_zl) * ROWS + (col & 15)
    row = lax.broadcasted_iota(jnp.int32, (128, 1), 0)
    parts = [jnp.zeros((1, 512), F32) for _ in range(3)]
    for first in (4, 2, 6, 0):
        row_y = (y + first + (row >> 6)) & 7
        row_zh = (zh + ((row >> 4) & 3)) & 3
        row_id = (x * 2 + zl) * 1024 + ((row_y * NZ + row_zh) * 2 + c) * ROWS + (row & 15)
        rows_y = YB[pl.ds(first, 2)].reshape(128, width)
        cols_x = XB[...].reshape(512, width)
        dots = lax.dot_general(rows_y, cols_x, (((1,), (1,)), ((), ())), preferred_element_type=F32)
        logits = temp_row * dots + shift
        match = row_id == col_id
        signed = jnp.where(match, -logits, logits)
        decay = jnp.exp(-jnp.abs(signed))
        total = 1.0 + decay
        loss = jnp.maximum(signed, 0.0) + jnp.log1p(decay)
        sig = jnp.where(signed >= 0, 1.0, decay) / total
        grad = jnp.where(match, -sig, sig)
        for n, value in enumerate((loss, grad * dots, grad)):
            parts[n] = parts[n] + jnp.sum(value, axis=0, keepdims=True)
        low = grad.astype(BF16)
        GT[pl.ds(first * 64, 128)] = low
        dy = jnp.dot(low, cols_x, preferred_element_type=F32).reshape(2, NZ, ROWS, width)
        DYF[pl.ds(first, 2)] = dy
        DYB[pl.ds(first, 2)] = dy.astype(BF16)

        @pl.when(c == 0)
        def _():
            for j in (first, first + 1):
                if j:
                    send(f"dy{j}", lambda j=j: DYB.at[j], lambda j=j: RY.at[j - 1], dict(dy=j), 0)

    @pl.when(c == 1)
    def _():
        for m in (2, 1, 3):
            send(f"dz{m}", lambda m=m: DYB.at[:, m], lambda m=m: RZ1.at[m - 1], dict(dz=m), 1)

    folded = [part[:, 0:128] + part[:, 128:256] + part[:, 256:384] + part[:, 384:512] for part in parts]
    PA[0] = jnp.concatenate(folded + [jnp.zeros((5, 128), F32)], axis=0)
    for j in FAR_FIRST:
        send(f"pa{j}", lambda j=j: PA.at[0], lambda j=j: PA.at[NX - j], dict(dx=j))

    texts_all = YB[...].reshape(512, width)
    over_texts = (((0,), (0,)), ((), ()))
    DXS[...] = lax.dot_general(GT[:, 256:512], texts_all, over_texts, preferred_element_type=F32).reshape(NX, 2, ROWS, width)
    for k in (4, 2, 6, 0):
        send(f"sx{k}", lambda k=k: DXS.at[pl.ds(k, 2)], lambda k=k: RXS.at[pl.ds(k, 2)], dict(dc=1))
    DX0[...] = lax.dot_general(GT[:, 0:256], texts_all, over_texts, preferred_element_type=F32).reshape(NX, 2, ROWS, width)
    for k in (4, 2, 6, 0):
        wait(f"sx{k}")
        both = DX0[pl.ds(k, 2)] + RXS[pl.ds(k, 2)]
        DXB[pl.ds(k, 2)] = both.astype(BF16)
        if k == 0:
            DXT[...] = both[0]
        for j in (k, k + 1):
            if j:
                send(f"dx{j}", lambda j=j: DXB.at[j], lambda j=j: RX.at[j - 1], dict(dx=j))

    for j in (1, 7, 2, 6, 3, 5, 4):
        wait(f"pa{j}")
    total = PA[(0 - x) % NX]
    for a in range(1, NX):
        total = total + PA[(a - x) % NX]
    PB[0] = total
    for j in FAR_FIRST:
        send(f"pb{j}", lambda j=j: PB.at[0], lambda j=j: PB.at[NY - j], dict(dy=j))

    @pl.when(c == 0)
    def _():
        for j in (1, 7, 2, 6, 3, 5, 4):
            wait(f"dy{j}")
        for m in (2, 1, 3, 0):
            part = DYF[0, m]
            for j in range(1, NY):
                part = part + RY[j - 1, m].astype(F32)
            TOT[m] = part
            if m:
                send(f"ez{m}", lambda m=m: TOT.at[m], lambda m=m: RZ.at[m - 1], dict(dz=m), 0)

    @pl.when(c == 1)
    def _():
        for m in (1, 3, 2):
            wait(f"dz{m}")
        for j in FAR_FIRST + (0,):
            part = DYF[j, 0]
            for m in range(1, NZ):
                part = part + RZ1[m - 1, j].astype(F32)
            TOT[j] = part
            if j:
                send(f"ey{j}", lambda j=j: TOT.at[j], lambda j=j: RY1.at[j - 1], dict(dy=j), 1)

    for j in (1, 7, 2, 6, 3, 5, 4):
        wait(f"pb{j}")
    total = PB[(0 - y) % NY]
    for a in range(1, NY):
        total = total + PB[(a - y) % NY]
    PC[0] = total
    for m in range(NZ):
        for a in (0, 1):
            for b in (0, 1):
                if (m, a, b) != (0, 0, 0):
                    send(f"pc{m}{a}{b}", lambda m=m, a=a, b=b: PC.at[0], lambda m=m, a=a, b=b: PC.at[((NZ - m) % NZ) * 4 + a * 2 + b], dict(dz=m, dl=a, dc=b))

    for j in (1, 7, 2, 6, 3, 5, 4):
        wait(f"dx{j}")
    part = DXT[1]
    for j in range(1, NX):
        part = part + RX[j - 1, 1].astype(F32)
    DXT[1] = part
    send("ex", lambda: DXT.at[1], lambda: RXZ, dict(dl=1))
    part = DXT[0]
    for j in range(1, NX):
        part = part + RX[j - 1, 0].astype(F32)
    DXT[0] = part

    for m in range(NZ):
        for a in (0, 1):
            for b in (0, 1):
                if (m, a, b) != (0, 0, 0):
                    wait(f"pc{m}{a}{b}")
    total = None
    for m in range(NZ):
        for a in (0, 1):
            for b in (0, 1):
                term = PC[((m - zh) % NZ) * 4 + ((a - zl) % 2) * 2 + (b - c) % 2]
                total = term if total is None else total + term
    batch = float(images_ref.shape[0] * NX * NY * NZ * 4)
    loss_ref[0] = jnp.sum(total[0:1]) / batch
    grad_temp_ref[0] = jnp.sum(temp * total[1:2]) / batch
    grad_bias_ref[0] = jnp.sum(total[2:3]) / batch

    scale = jnp.exp(jnp.full((1, width), log_temp_ref[0], F32))

    @pl.when(c == 0)
    def _():
        part = TOT[0]
        for m in range(1, NZ):
            wait(f"ez{m}")
            part = part + RZ[m - 1]
        DYN[...] = part

    @pl.when(c == 1)
    def _():
        part = TOT[0]
        for j in range(1, NY):
            wait(f"ey{j}")
            part = part + RY1[j - 1]
        DYN[...] = part

    grad_texts_ref[...] = unnormalize(y_norm, inv_y, scale * DYN[...])
    wait("ex")
    grad_images_ref[...] = unnormalize(x_norm, inv_x, scale * (DXT[0] + RXZ[...]))

    for name in sends["all"]:
        copy_of(name).wait_send()
    for core in (0, 1):

        @pl.when(c == core)
        def _():
            for name in sends[core]:
                copy_of(name).wait_send()


def body(images, texts, log_temp, bias):
    rows, width = images.shape
    smem = pl.BlockSpec(memory_space=pltpu.SMEM)
    vmem = pl.BlockSpec(memory_space=pltpu.VMEM)
    scalar = jax.ShapeDtypeStruct((1,), F32)
    wide = jax.ShapeDtypeStruct((rows, width), F32)
    piece = (rows, width)
    scratch = [
        ((2, NX, 2) + piece, BF16),
        ((NY, NZ) + piece, BF16),
        ((512, 512), BF16),
        ((NY, NZ) + piece, F32),
        ((NY, NZ) + piece, BF16),
        ((NY - 1, NZ) + piece, BF16),
        ((NZ - 1,) + piece, F32),
        ((NZ - 1, NY) + piece, BF16),
        ((NY - 1,) + piece, F32),
        ((NY,) + piece, F32),
        (piece, F32),
        ((NX, 2) + piece, F32),
        ((NX, 2) + piece, F32),
        ((NX, 2) + piece, F32),
        ((NX, 2) + piece, BF16),
        ((NX - 1, 2) + piece, BF16),
        (piece, F32),
        ((2,) + piece, F32),
        ((NX, 8, 128), F32),
        ((NY, 8, 128), F32),
        ((16, 8, 128), F32),
    ]
    return pl.pallas_call(
        kernel,
        out_shape=(scalar, wide, wide, scalar, scalar),
        in_specs=[smem, smem, vmem, vmem],
        out_specs=(smem, vmem, vmem, smem, smem),
        scratch_shapes=[pltpu.VMEM(shape, kind) for shape, kind in scratch]
        + [pltpu.SemaphoreType.DMA((128,)), pltpu.SemaphoreType.DMA((128,))],
        compiler_params=pltpu.CompilerParams(collective_id=0, has_side_effects=True, vmem_limit_bytes=48 * 2**20),
        name="sigmoid_loss",
    )(log_temp, bias, images, texts)


def solution(mesh):
    in_specs = (P(("img", "txt"), None), P(("txt", "img"), None), P(), P())
    out_specs = (P(), P(("img", "txt"), None), P(("txt", "img"), None), P(), P())
    return jax.shard_map(body, mesh=mesh, in_specs=in_specs, out_specs=out_specs, check_vma=False)
```

```python
import jax
import jax.numpy as jnp
from jax import lax
from jax.experimental import pallas as pl
from jax.experimental.pallas import tpu as pltpu
from jax.sharding import PartitionSpec as P

MESH = pl.DeviceIdType.MESH
F32, BF16 = jnp.float32, jnp.bfloat16
NX, NY, NZ = 8, 8, 4
ROWS = 16
VMEM_LIMIT = 48 * 2**20
FAR_FIRST = (4, 3, 5, 2, 6, 1, 7)
NEAR_FIRST = (1, 7, 2, 6, 3, 5, 4)
LAST_Z = {4: (1, 3, 2), 3: (1, 3), 5: (1, 3), 2: (1,), 6: (3,)}
LAST_Y = {1: (1, 3), 7: (1, 3), 3: (2, 1), 5: (2, 1), 2: (2, 2), 6: (1, 2)}
FAR = (3, 4, 5)
NEAR = (1, 7, 2, 6)


def normalize(embed):
    wide = embed.astype(F32)
    inverse = lax.rsqrt(jnp.sum(wide * wide, axis=-1, keepdims=True) + 1e-06)
    return wide * inverse, inverse


def unnormalize(normed, inverse, grad_normed):
    inner = jnp.sum(normed * grad_normed, axis=-1, keepdims=True)
    return inverse * (grad_normed - normed * inner)


def kernel(
    log_temp_ref, bias_ref, images_ref, texts_ref,
    grad_images_ref, grad_texts_ref, sums_ref,
    XB, YB, GT, DYF, DYB, RY, RZ1, RY1, RZ, DYO, DXS, RXS, DX0, DXB, RX, RXL, RX2, RXZ, PA, PB, PC,
    ss, rs,
):
    img, txt = lax.axis_index("img"), lax.axis_index("txt")
    y, zh, c = img // (NZ * 2), (img // 2) % NZ, img % 2
    x, zl = txt // 2, txt % 2
    width = images_ref.shape[1]

    def device(dx=0, dy=0, dz=0, dl=0, dc=0):
        i = ((((y + dy) % NY) * NZ + (zh + dz) % NZ) * 2) + (c + dc) % 2
        t = ((x + dx) % NX) * 2 + (zl + dl) % 2
        return (i, t)

    sent = {}

    def send(name, src, dst, **to):
        q = len(sent)
        sent[name] = pltpu.make_async_remote_copy(
            src_ref=src, dst_ref=dst, send_sem=ss.at[q], recv_sem=rs.at[q],
            device_id=device(**to), device_id_type=MESH,
        )
        sent[name].start()

    def wait(name):
        sent[name].wait_recv()

    others = [dict(dz=m, dl=a, dc=b) for m in range(NZ) for a in (0, 1) for b in (0, 1) if (m, a, b) != (0, 0, 0)]
    peers = [dict(dx=j) for j in range(1, NX)] + [dict(dy=j) for j in range(1, NY)] + others
    barrier = pltpu.get_barrier_semaphore()
    for peer in peers:
        pl.semaphore_signal(barrier, inc=1, device_id=device(**peer), device_id_type=MESH)

    x_norm, inv_x = normalize(images_ref[...])
    y_norm, inv_y = normalize(texts_ref[...])
    XB[0, 0, 0] = x_norm.astype(BF16)
    YB[0, 0] = y_norm.astype(BF16)
    pl.semaphore_wait(barrier, len(peers))

    for m in (1, 3, 2):
        send(f"tz{NZ - m}", YB.at[0, 0], YB.at[0, NZ - m], dz=m)
    send("xl", XB.at[0, 0, 0], XB.at[0, 0, 1], dl=1)
    for j in FAR_FIRST:
        send(f"ty{NY - j}", YB.at[0, 0], YB.at[NY - j, 0], dy=j)
        send(f"xo{NX - j}", XB.at[0, 0, 0], XB.at[0, NX - j, 0], dx=j)
    wait("xl")
    for k in (2, 6, 1, 7):
        send(f"xp{k}", XB.at[0, 0, 1], XB.at[0, k, 1], dx=NX - k)
    for r in (1, 3, 2):
        wait(f"tz{r}")
    for k in (1, 7, 3, 5):
        r, n = LAST_Y[k]
        send(f"tp{k}", YB.at[0, pl.ds(r, n)], YB.at[k, pl.ds(r, n)], dy=NY - k)
    send("xs0", XB.at[0, 0], XB.at[1, 0], dc=1)
    for k, rs_of in LAST_Z.items():
        wait(f"ty{k}")
        for r in rs_of:
            send(f"tw{k}{r}", YB.at[k, 0], YB.at[k, r], dz=NZ - r)
        if k in FAR:
            wait(f"xo{k}")
            send(f"xq{k}", XB.at[0, k, 0], XB.at[0, k, 1], dl=1)
    for k, near, to in ((2, 1, NY - 1), (6, 7, 1)):
        r, n = LAST_Y[k]
        wait(f"tp{near}")
        send(f"tp{k}", YB.at[near, pl.ds(r, n)], YB.at[k, pl.ds(r, n)], dy=to)
    for k in (1, 2):
        wait(f"xo{k}")
        wait(f"xp{k}")
    send("xs1", XB.at[0, pl.ds(1, 2)], XB.at[1, pl.ds(1, 2)], dc=1)
    for k in (6, 7):
        wait(f"xo{k}")
        wait(f"xp{k}")
    send("xs6", XB.at[0, pl.ds(6, 2)], XB.at[1, pl.ds(6, 2)], dc=1)
    for k in FAR:
        wait(f"xq{k}")
    send("xs3", XB.at[0, pl.ds(3, 3)], XB.at[1, pl.ds(3, 3)], dc=1)
    for k in (1, 7):
        wait(f"ty{k}")
    for k in (0, 1, 6, 3):
        wait(f"xs{k}")

    temp_row = jnp.exp(jnp.full((1, 512), log_temp_ref[0], F32))
    shift = bias_ref[0]
    col = lax.broadcasted_iota(jnp.int32, (1, 512), 1)
    col_core = (c + (col >> 8)) & 1
    col_x = (x + ((col >> 5) & 7)) & 7
    col_zl = (zl + ((col >> 4) & 1)) & 1
    col_id = ((y * NZ + zh) * 2 + col_core) * 256 + (col_x * 2 + col_zl) * ROWS + (col & 15)
    row = lax.broadcasted_iota(jnp.int32, (128, 1), 0)
    parts = [jnp.zeros((1, 512), F32) for _ in range(3)]

    def text_product(first):
        cols_x = XB[...].reshape(512, width)
        dy = jnp.dot(GT[pl.ds(first * 64, 128)], cols_x, preferred_element_type=F32).reshape(2, NZ, ROWS, width)
        DYF[pl.ds(first, 2)] = dy
        DYB[pl.ds(first, 2)] = dy.astype(BF16)

    def send_dy(first):
        for k in (first, first + 1):
            for r in LAST_Z.get(k, ()):
                send(f"dz{k}{r}", DYB.at[k, r], RZ1.at[k, r], dz=r)
        for k in (first, first + 1):
            if k in LAST_Y:
                r, n = LAST_Y[k]
                send(f"dy{k}", DYB.at[k, pl.ds(r, n)], RY.at[k, pl.ds(r, n)], dy=k)

    for first in (0, 6, 2, 4):
        for k in (first, first + 1):
            if k in (2, 3, 5, 6):
                wait(f"tp{k}")
            for r in LAST_Z.get(k, ()):
                wait(f"tw{k}{r}")
        row_y = (y + first + (row >> 6)) & 7
        row_zh = (zh + ((row >> 4) & 3)) & 3
        row_id = (x * 2 + zl) * 1024 + ((row_y * NZ + row_zh) * 2 + c) * ROWS + (row & 15)
        rows_y = YB[pl.ds(first, 2)].reshape(128, width)
        cols_x = XB[...].reshape(512, width)
        dots = lax.dot_general(rows_y, cols_x, (((1,), (1,)), ((), ())), preferred_element_type=F32)
        logits = temp_row * dots + shift
        match = row_id == col_id
        signed = jnp.where(match, -logits, logits)
        decay = jnp.exp(-jnp.abs(signed))
        loss = jnp.maximum(signed, 0.0) + jnp.log1p(decay)
        sig = jnp.where(signed >= 0, 1.0, decay) / (1.0 + decay)
        grad = jnp.where(match, -sig, sig)
        for n, value in enumerate((loss, grad * dots, grad)):
            parts[n] = parts[n] + jnp.sum(value, axis=0, keepdims=True)
        GT[pl.ds(first * 64, 128)] = grad.astype(BF16)
        if first != 4:
            text_product(first)
            send_dy(first)

    folded = [part[:, 0:128] + part[:, 128:256] + part[:, 256:384] + part[:, 384:512] for part in parts]
    PA[0] = jnp.concatenate(folded + [jnp.zeros((5, 128), F32)], axis=0)

    text_product(4)
    send_dy(4)
    texts_all = YB[...].reshape(512, width)
    over_texts = (((0,), (0,)), ((), ()))
    DXS[...] = lax.dot_general(GT[:, 256:512], texts_all, over_texts, preferred_element_type=F32).reshape(NX, 2, ROWS, width)
    for k, n in ((3, 3), (1, 2), (6, 2), (0, 1)):
        send(f"sx{k}", DXS.at[pl.ds(k, n)], RXS.at[pl.ds(k, n)], dc=1)
    DX0[...] = lax.dot_general(GT[:, 0:256], texts_all, over_texts, preferred_element_type=F32).reshape(NX, 2, ROWS, width)
    for j in FAR_FIRST:
        send(f"pa{NX - j}", PA.at[0], PA.at[NX - j], dx=j)
    for k in (1, 7):
        send(f"do{k}", DYB.at[k, 0], RY.at[k, 0], dy=k)
    for k, n in ((3, 3), (1, 2), (6, 2), (0, 1)):
        wait(f"sx{k}")
        both = DX0[pl.ds(k, n)] + RXS[pl.ds(k, n)]
        DX0[pl.ds(k, n)] = both
        DXB[pl.ds(k, n)] = both.astype(BF16)
        if k == 3:
            send("dl", DXB.at[pl.ds(3, 3), 1], RXL, dl=1)
        elif k:
            for j in (k, k + 1):
                send(f"dx{j}", DXB.at[j], RX.at[j], dx=j)

    def wide(ref):
        return ref.astype(F32)

    for k in range(1, NX):
        wait(f"pa{k}")
    total = PA[(0 - x) % NX]
    for a in range(1, NX):
        total = total + PA[(a - x) % NX]
    PB[0] = total
    for j in FAR_FIRST:
        send(f"pb{NY - j}", PB.at[0], PB.at[NY - j], dy=j)

    wait("dl")
    for n, k in enumerate(FAR):
        DXB[k, 0] = (DX0[k, 0] + wide(RXL[n])).astype(BF16)
        send(f"ex{k}", DXB.at[k, 0], RX2.at[n], dx=k)

    for n, (k, rows) in enumerate(LAST_Z.items()):
        part = DYF[k, 0]
        for r in rows:
            wait(f"dz{k}{r}")
            part = part + wide(RZ1[k, r])
        DYB[k, 0] = part.astype(BF16)
        send(f"ey{k}", DYB.at[k, 0], RY1.at[n], dy=k)

    for k in range(1, NY):
        wait(f"pb{k}")
    total = PB[(0 - y) % NY]
    for a in range(1, NY):
        total = total + PB[(a - y) % NY]
    PC[0] = total
    for to in others:
        m, a, b = to["dz"], to["dl"], to["dc"]
        slot = ((NZ - m) % NZ) * 4 + a * 2 + b
        send(f"pc{slot}", PC.at[0], PC.at[slot], **to)

    for k in NEAR:
        wait(f"dx{k}")
    part = DX0[0, 1]
    for k in NEAR:
        part = part + wide(RX[k, 1])
    DXB[0, 1] = part.astype(BF16)
    send("el", DXB.at[0, 1], RXZ, dl=1)

    for k in LAST_Y:
        wait(f"dy{k}")
    for r in (2, 1, 3):
        part = DYF[0, r]
        for k, (low, n) in LAST_Y.items():
            if low <= r < low + n:
                part = part + wide(RY[k, r])
        DYB[0, r] = part.astype(BF16)
        send(f"ez{r}", DYB.at[0, r], RZ.at[r - 1], dz=r)

    part = DYF[0, 0]
    for k in (1, 7):
        wait(f"do{k}")
        part = part + wide(RY[k, 0])
    DYO[...] = part
    part = DX0[0, 0]
    for k in NEAR:
        part = part + wide(RX[k, 0])
    DX0[0, 0] = part

    scale = jnp.exp(jnp.full((1, width), log_temp_ref[0], F32))
    x_norm, inv_x = normalize(images_ref[...])
    wait("el")
    part = DX0[0, 0] + wide(RXZ[...])
    for n, k in enumerate(FAR):
        wait(f"ex{k}")
        part = part + wide(RX2[n])
    grad_images_ref[...] = unnormalize(x_norm, inv_x, scale * part)

    y_norm, inv_y = normalize(texts_ref[...])
    part = DYO[...]
    for r in (1, 3, 2):
        wait(f"ez{r}")
        part = part + wide(RZ[r - 1])
    for n, k in enumerate(LAST_Z):
        wait(f"ey{k}")
        part = part + wide(RY1[n])
    grad_texts_ref[...] = unnormalize(y_norm, inv_y, scale * part)

    for slot in range(1, 16):
        wait(f"pc{slot}")
    total = None
    for m in range(NZ):
        for a in (0, 1):
            for b in (0, 1):
                term = PC[((m - zh) % NZ) * 4 + ((a - zl) % 2) * 2 + (b - c) % 2]
                total = term if total is None else total + term
    batch = float(images_ref.shape[0] * NX * NY * NZ * 4)
    temp = jnp.exp(jnp.full((1, 128), log_temp_ref[0], F32))
    sums_ref[...] = jnp.concatenate([total[0:1], temp * total[1:2], total[2:8]], axis=0) / batch

    for copy in sent.values():
        copy.wait_send()


def finish(
    grad_images_ref, grad_texts_ref, sums_ref,
    loss_out, grad_images_out, grad_texts_out, grad_temp_out, grad_bias_out,
    loss_ref, grad_temp_ref, grad_bias_ref, sems,
):
    copies = [
        pltpu.make_async_copy(src, dst, sems.at[n])
        for n, (src, dst) in enumerate(
            (
                (grad_images_ref, grad_images_out), (grad_texts_ref, grad_texts_out),
                (loss_ref, loss_out), (grad_temp_ref, grad_temp_out), (grad_bias_ref, grad_bias_out),
            )
        )
    ]
    for copy in copies[:2]:
        copy.start()
    loss_ref[0] = jnp.sum(sums_ref[0:1])
    grad_temp_ref[0] = jnp.sum(sums_ref[1:2])
    grad_bias_ref[0] = jnp.sum(sums_ref[2:3])
    for copy in copies[2:]:
        copy.start()
    for copy in copies:
        copy.wait()


def body(images, texts, log_temp, bias):
    rows, width = images.shape
    smem = pl.BlockSpec(memory_space=pltpu.SMEM)
    anywhere = pl.BlockSpec(memory_space=pl.ANY)
    scalar = jax.ShapeDtypeStruct((1,), F32)
    vmem = pl.BlockSpec(memory_space=pltpu.VMEM)
    wide = jax.ShapeDtypeStruct((rows, width), F32)
    piece = (rows, width)
    scratch = [
        ((2, NX, 2) + piece, BF16),
        ((NY, NZ) + piece, BF16),
        ((512, 512), BF16),
        ((NY, NZ) + piece, F32),
        ((NY, NZ) + piece, BF16),
        ((NY, NZ) + piece, BF16),
        ((7, NZ) + piece, BF16),
        ((5,) + piece, BF16),
        ((3,) + piece, BF16),
        (piece, F32),
        ((NX, 2) + piece, F32),
        ((NX, 2) + piece, F32),
        ((NX, 2) + piece, F32),
        ((NX, 2) + piece, BF16),
        ((NX, 2) + piece, BF16),
        ((3,) + piece, BF16),
        ((3,) + piece, BF16),
        (piece, BF16),
        ((NX, 8, 128), F32),
        ((NY, 8, 128), F32),
        ((16, 8, 128), F32),
    ]
    dma = pltpu.SemaphoreType.DMA
    grad_images, grad_texts, sums = pl.pallas_call(
        kernel,
        out_shape=(wide, wide, jax.ShapeDtypeStruct((8, 128), F32)),
        in_specs=[smem, smem, vmem, vmem],
        out_specs=(vmem, vmem, vmem),
        scratch_shapes=[pltpu.VMEM(shape, kind) for shape, kind in scratch] + [dma((128,)), dma((128,))],
        compiler_params=pltpu.CompilerParams(collective_id=0, has_side_effects=True, vmem_limit_bytes=VMEM_LIMIT),
        name="sigmoid_loss",
    )(log_temp, bias, images, texts)
    return pl.pallas_call(
        finish,
        out_shape=(scalar, wide, wide, scalar, scalar),
        in_specs=[vmem] * 3,
        out_specs=(anywhere,) * 5,
        scratch_shapes=[pltpu.SMEM((1,), F32)] * 3 + [dma((5,))],
        compiler_params=pltpu.CompilerParams(vmem_limit_bytes=2**20),
        name="write_out",
    )(grad_images, grad_texts, sums)


def solution(mesh):
    in_specs = (P(("img", "txt"), None), P(("txt", "img"), None), P(), P())
    out_specs = (P(), P(("img", "txt"), None), P(("txt", "img"), None), P(), P())
    return jax.shard_map(body, mesh=mesh, in_specs=in_specs, out_specs=out_specs, check_vma=False)
```

```python
import jax
import jax.numpy as jnp
from jax import lax
from jax.experimental import pallas as pl
from jax.experimental.pallas import tpu as pltpu
from jax.sharding import PartitionSpec as P

MESH = pl.DeviceIdType.MESH
F32, BF16 = jnp.float32, jnp.bfloat16
NX, NY, NZ = 8, 8, 4
ROWS = 16
VMEM_LIMIT = 48 * 2**20
FAR_FIRST = (4, 3, 5, 2, 6, 1, 7)
NEAR_FIRST = (1, 7, 2, 6, 3, 5, 4)
LAST_Z = {4: (1, 3, 2), 3: (1, 3), 5: (1, 3)}
LAST_Y = {1: (1, 3), 7: (1, 3), 3: (2, 1), 5: (2, 1), 2: (1, 3), 6: (1, 3)}
FAR = (3, 4, 5)
NEAR = (2, 6, 1, 7)
ALONG_X = (3, 5, 2, 6, 1, 7)


def normalize(embed):
    wide = embed.astype(F32)
    inverse = lax.rsqrt(jnp.sum(wide * wide, axis=-1, keepdims=True) + 1e-06)
    return wide * inverse, inverse


def unnormalize(normed, inverse, grad_normed):
    inner = jnp.sum(normed * grad_normed, axis=-1, keepdims=True)
    return inverse * (grad_normed - normed * inner)


def kernel(
    given_ref,
    grad_images_ref, grad_texts_ref, sums_ref,
    XB, YB, GT, DYF, DYB, RY, RZ1, RY1, RZ, DYO, DXS, RXS, DX0, DXB, RX, RXL, RXZ, PA, PB, PC,
    ss, rs,
):
    img, txt = lax.axis_index("img"), lax.axis_index("txt")
    y, zh, c = img // (NZ * 2), (img // 2) % NZ, img % 2
    x, zl = txt // 2, txt % 2
    width = given_ref.shape[1]
    images_ref, texts_ref = given_ref.at[0:ROWS], given_ref.at[ROWS : 2 * ROWS]

    def device(dx=0, dy=0, dz=0, dl=0, dc=0):
        i = ((((y + dy) % NY) * NZ + (zh + dz) % NZ) * 2) + (c + dc) % 2
        t = ((x + dx) % NX) * 2 + (zl + dl) % 2
        return (i, t)

    sent = {}

    def send(name, src, dst, **to):
        q = len(sent)
        sent[name] = pltpu.make_async_remote_copy(
            src_ref=src, dst_ref=dst, send_sem=ss.at[q], recv_sem=rs.at[q],
            device_id=device(**to), device_id_type=MESH,
        )
        sent[name].start()

    def wait(name):
        sent[name].wait_recv()

    drained = set()

    def drain(*kinds):
        for name, copy in sent.items():
            if name not in drained and name.startswith(kinds):
                drained.add(name)
                copy.wait_send()

    others = [dict(dz=m, dl=a, dc=b) for m in range(NZ) for a in (0, 1) for b in (0, 1) if (m, a, b) != (0, 0, 0)]
    peers = [dict(dx=j) for j in range(1, NX)] + [dict(dy=j) for j in range(1, NY)] + others
    barrier = pltpu.get_barrier_semaphore()
    for peer in peers:
        pl.semaphore_signal(barrier, inc=1, device_id=device(**peer), device_id_type=MESH)

    x_norm, inv_x = normalize(images_ref[...])
    y_norm, inv_y = normalize(texts_ref[...])
    XB[0, 0, 0] = x_norm.astype(BF16)
    YB[0, 0] = y_norm.astype(BF16)
    pl.semaphore_wait(barrier, len(peers))

    for m in (1, 3, 2):
        send(f"tz{NZ - m}", YB.at[0, 0], YB.at[0, NZ - m], dz=m)
    send("xl", XB.at[0, 0, 0], XB.at[0, 0, 1], dl=1)
    for j in (6, 2, 4):
        send(f"ty{NY - j}", YB.at[0, 0], YB.at[NY - j, 0], dy=j)
    for j in (4, 3, 5):
        send(f"xo{NX - j}", XB.at[0, 0, 0], XB.at[0, NX - j, 0], dx=j)
    for j in (1, 7):
        send(f"ty{NY - j}", YB.at[0, 0], YB.at[NY - j, 0], dy=j)
    for j in (2, 6, 1, 7):
        send(f"xo{NX - j}", XB.at[0, 0, 0], XB.at[0, NX - j, 0], dx=j)
    wait("xl")
    for k in (2, 6, 1, 7):
        send(f"xp{k}", XB.at[0, 0, 1], XB.at[0, k, 1], dx=NX - k)
    for k, near, to in ((3, 2, NY - 1), (5, 6, 1)):
        wait(f"ty{near}")
        send(f"ty{k}", YB.at[near, 0], YB.at[k, 0], dy=to)
    for r in (1, 3, 2):
        wait(f"tz{r}")
    for k in (1, 7, 3, 5):
        r, n = LAST_Y[k]
        send(f"tp{k}", YB.at[0, pl.ds(r, n)], YB.at[k, pl.ds(r, n)], dy=NY - k)
    send("xs0", XB.at[0, 0], XB.at[1, 0], dc=1)
    for k in (4, 3, 5):
        wait(f"xo{k}")
        send(f"xq{k}", XB.at[0, k, 0], XB.at[0, k, 1], dl=1)
    for k, rows in LAST_Z.items():
        wait(f"ty{k}")
        for r in rows:
            send(f"tw{k}{r}", YB.at[k, 0], YB.at[k, r], dz=NZ - r)
    for k, near, to in ((2, 1, NY - 1), (6, 7, 1)):
        r, n = LAST_Y[k]
        wait(f"tp{near}")
        send(f"tp{k}", YB.at[near, pl.ds(r, n)], YB.at[k, pl.ds(r, n)], dy=to)
    for k in (1, 2):
        wait(f"xo{k}")
        wait(f"xp{k}")
    send("xs1", XB.at[0, pl.ds(1, 2)], XB.at[1, pl.ds(1, 2)], dc=1)
    for k in (6, 7):
        wait(f"xo{k}")
        wait(f"xp{k}")
    send("xs6", XB.at[0, pl.ds(6, 2)], XB.at[1, pl.ds(6, 2)], dc=1)
    for k in FAR:
        wait(f"xq{k}")
    send("xs3", XB.at[0, pl.ds(3, 3)], XB.at[1, pl.ds(3, 3)], dc=1)
    for k in (1, 7):
        wait(f"ty{k}")
    for k in (0, 1, 6, 3):
        wait(f"xs{k}")

    temp_row = jnp.exp(given_ref[2 * ROWS : 2 * ROWS + 1, 0:512])
    shift_row = given_ref[2 * ROWS + 1 : 2 * ROWS + 2, 0:512]
    col = lax.broadcasted_iota(jnp.int32, (1, 512), 1)
    col_core = (c + (col >> 8)) & 1
    col_x = (x + ((col >> 5) & 7)) & 7
    col_zl = (zl + ((col >> 4) & 1)) & 1
    col_id = ((y * NZ + zh) * 2 + col_core) * 256 + (col_x * 2 + col_zl) * ROWS + (col & 15)
    row = lax.broadcasted_iota(jnp.int32, (128, 1), 0)
    parts = [jnp.zeros((1, 512), F32) for _ in range(3)]

    def text_product(first):
        cols_x = XB[...].reshape(512, width)
        dy = jnp.dot(GT[pl.ds(first * 64, 128)], cols_x, preferred_element_type=F32).reshape(2, NZ, ROWS, width)
        DYF[pl.ds(first, 2)] = dy
        DYB[pl.ds(first, 2)] = dy.astype(BF16)

    def send_dy(first):
        for k in (first, first + 1):
            for r in LAST_Z.get(k, ()):
                send(f"dz{k}{r}", DYB.at[k, r], RZ1.at[k, r], dz=r)
        for k in (first, first + 1):
            if k in LAST_Y:
                r, n = LAST_Y[k]
                send(f"dy{k}", DYB.at[k, pl.ds(r, n)], RY.at[k, pl.ds(r, n)], dy=k)

    for first in (0, 4, 2, 6):
        for k in (first, first + 1):
            if k in (2, 3, 5, 6):
                wait(f"tp{k}")
            for r in LAST_Z.get(k, ()):
                wait(f"tw{k}{r}")
        row_y = (y + first + (row >> 6)) & 7
        row_zh = (zh + ((row >> 4) & 3)) & 3
        row_id = (x * 2 + zl) * 1024 + ((row_y * NZ + row_zh) * 2 + c) * ROWS + (row & 15)
        rows_y = YB[pl.ds(first, 2)].reshape(128, width)
        cols_x = XB[...].reshape(512, width)
        dots = lax.dot_general(rows_y, cols_x, (((1,), (1,)), ((), ())), preferred_element_type=F32)
        logits = temp_row * dots + shift_row
        match = row_id == col_id
        signed = jnp.where(match, -logits, logits)
        decay = jnp.exp(-jnp.abs(signed))
        loss = jnp.maximum(signed, 0.0) + jnp.log1p(decay)
        sig = jnp.where(signed >= 0, 1.0, decay) / (1.0 + decay)
        grad = jnp.where(match, -sig, sig)
        for n, value in enumerate((loss, grad * dots, grad)):
            parts[n] = parts[n] + jnp.sum(value, axis=0, keepdims=True)
        GT[pl.ds(first * 64, 128)] = grad.astype(BF16)
        if first != 6:
            text_product(first)
            send_dy(first)

    folded = [part[:, 0:128] + part[:, 128:256] + part[:, 256:384] + part[:, 384:512] for part in parts]
    PA[0] = jnp.concatenate(folded + [jnp.zeros((5, 128), F32)], axis=0)

    texts_all = YB[...].reshape(512, width)
    over_texts = (((0,), (0,)), ((), ()))
    groups = ((4, 4), (0, 4))
    for first, n in groups:
        rows = pl.ds(256 + first * 32, n * 32)
        DXS[pl.ds(first, n)] = lax.dot_general(
            GT[:, rows], texts_all, over_texts, preferred_element_type=F32
        ).reshape(n, 2, ROWS, width)
        send(f"sx{first}", DXS.at[pl.ds(first, n)], RXS.at[pl.ds(first, n)], dc=1)
    text_product(6)
    send_dy(6)
    for j in FAR_FIRST:
        send(f"pa{NX - j}", PA.at[0], PA.at[NX - j], dx=j)
    DX0[...] = lax.dot_general(GT[:, 0:256], texts_all, over_texts, preferred_element_type=F32).reshape(NX, 2, ROWS, width)
    for first, n in groups:
        wait(f"sx{first}")
        both = DX0[pl.ds(first, n)] + RXS[pl.ds(first, n)]
        DX0[pl.ds(first, n)] = both
        DXB[pl.ds(first, n)] = both.astype(BF16)
        for k in range(first, first + n):
            if k == 4:
                send("dl", DXB.at[4, 1], RXL, dl=1)
            elif k:
                send(f"dp{k}", DXB.at[k, 1], RX.at[k, 1], dx=k)
    for k in ALONG_X:
        send(f"dx{k}", DXB.at[k, 0], RX.at[k, 0], dx=k)

    def wide(ref):
        return ref.astype(F32)

    drain("t", "xl", "xo", "xp", "xq", "xs")

    for k in range(1, NX):
        wait(f"pa{k}")
    total = PA[(0 - x) % NX]
    for a in range(1, NX):
        total = total + PA[(a - x) % NX]
    PB[0] = total
    for to in others:
        m, a, b = to["dz"], to["dl"], to["dc"]
        slot = ((NZ - m) % NZ) * 4 + a * 2 + b
        send(f"pb{slot}", PB.at[0], PB.at[slot], **to)

    for n, (k, rows) in enumerate(LAST_Z.items()):
        part = DYF[k, 0]
        for r in rows:
            wait(f"dz{k}{r}")
            part = part + wide(RZ1[k, r])
        DYB[k, 0] = part.astype(BF16)
        send(f"ey{k}", DYB.at[k, 0], RY1.at[n], dy=k)

    for k in NEAR:
        send(f"do{k}", DYB.at[k, 0], RY.at[k, 0], dy=k)

    wait("dl")
    DXB[4, 0] = (DX0[4, 0] + wide(RXL[...])).astype(BF16)
    send("ex", DXB.at[4, 0], RX.at[4, 0], dx=4)

    for k in LAST_Y:
        wait(f"dy{k}")
    for r in (2, 1, 3):
        part = DYF[0, r]
        for k, (low, n) in LAST_Y.items():
            if low <= r < low + n:
                part = part + wide(RY[k, r])
        DYB[0, r] = part.astype(BF16)
        send(f"ez{r}", DYB.at[0, r], RZ.at[r - 1], dz=r)

    drain("dz", "dy", "sx", "pa")

    part = DX0[0, 1]
    for k in ALONG_X:
        wait(f"dp{k}")
        part = part + wide(RX[k, 1])
    DXB[0, 1] = part.astype(BF16)
    send("el", DXB.at[0, 1], RXZ, dl=1)

    for slot in range(1, 16):
        wait(f"pb{slot}")
    total = None
    for m in range(NZ):
        for a in (0, 1):
            for b in (0, 1):
                term = PB[((m - zh) % NZ) * 4 + ((a - zl) % 2) * 2 + (b - c) % 2]
                total = term if total is None else total + term
    PC[0] = total
    for j in FAR_FIRST:
        send(f"pc{NY - j}", PC.at[0], PC.at[NY - j], dy=j)

    part = DYF[0, 0]
    for k in NEAR:
        wait(f"do{k}")
        part = part + wide(RY[k, 0])
    DYO[...] = part
    part = DX0[0, 0]
    for k in ALONG_X:
        wait(f"dx{k}")
        part = part + wide(RX[k, 0])
    DX0[0, 0] = part

    drain("pb", "dp", "dx", "dl", "do", "ey", "ex")
    scale = jnp.exp(given_ref[2 * ROWS : 2 * ROWS + 1])
    y_norm, inv_y = normalize(texts_ref[...])
    part = DYO[...]
    for r in (1, 3, 2):
        wait(f"ez{r}")
        part = part + wide(RZ[r - 1])
    for n, k in enumerate(LAST_Z):
        wait(f"ey{k}")
        part = part + wide(RY1[n])
    grad_texts_ref[...] = unnormalize(y_norm, inv_y, scale * part)

    x_norm, inv_x = normalize(images_ref[...])
    wait("el")
    part = DX0[0, 0] + wide(RXZ[...])
    wait("ex")
    part = part + wide(RX[4, 0])
    grad_images_ref[...] = unnormalize(x_norm, inv_x, scale * part)

    for k in range(1, NY):
        wait(f"pc{k}")
    total = PC[(0 - y) % NY]
    for a in range(1, NY):
        total = total + PC[(a - y) % NY]
    batch = float(ROWS * NX * NY * NZ * 4)
    temp = jnp.exp(given_ref[2 * ROWS : 2 * ROWS + 1, 0:128])
    sums_ref[...] = jnp.concatenate([total[0:1], temp * total[1:2], total[2:8]], axis=0) / batch

    drain("")


def finish(
    grad_images_ref, grad_texts_ref, sums_ref,
    loss_out, grad_images_out, grad_texts_out, grad_temp_out, grad_bias_out,
    loss_ref, grad_temp_ref, grad_bias_ref, sems,
):
    copies = [
        pltpu.make_async_copy(src, dst, sems.at[n])
        for n, (src, dst) in enumerate(
            (
                (grad_images_ref, grad_images_out), (grad_texts_ref, grad_texts_out),
                (loss_ref, loss_out), (grad_temp_ref, grad_temp_out), (grad_bias_ref, grad_bias_out),
            )
        )
    ]
    for copy in copies[:2]:
        copy.start()
    loss_ref[0] = jnp.sum(sums_ref[0:1])
    grad_temp_ref[0] = jnp.sum(sums_ref[1:2])
    grad_bias_ref[0] = jnp.sum(sums_ref[2:3])
    for copy in copies[2:]:
        copy.start()
    for copy in copies:
        copy.wait()


def body(images, texts, log_temp, bias):
    rows, width = images.shape
    anywhere = pl.BlockSpec(memory_space=pl.ANY)
    scalar = jax.ShapeDtypeStruct((1,), F32)
    vmem = pl.BlockSpec(memory_space=pltpu.VMEM)
    wide = jax.ShapeDtypeStruct((rows, width), F32)
    piece = (rows, width)
    scratch = [
        ((2, NX, 2) + piece, BF16),
        ((NY, NZ) + piece, BF16),
        ((512, 512), BF16),
        ((NY, NZ) + piece, F32),
        ((NY, NZ) + piece, BF16),
        ((NY, NZ) + piece, BF16),
        ((6, NZ) + piece, BF16),
        ((3,) + piece, BF16),
        ((3,) + piece, BF16),
        (piece, F32),
        ((NX, 2) + piece, F32),
        ((NX, 2) + piece, F32),
        ((NX, 2) + piece, F32),
        ((NX, 2) + piece, BF16),
        ((NX, 2) + piece, BF16),
        (piece, BF16),
        (piece, BF16),
        ((NX, 8, 128), F32),
        ((16, 8, 128), F32),
        ((NY, 8, 128), F32),
    ]
    dma = pltpu.SemaphoreType.DMA
    scalars = jnp.concatenate([jnp.broadcast_to(v[0], (1, width)) for v in (log_temp, bias)] + [jnp.zeros((6, width), F32)])
    given = jnp.concatenate([images.astype(F32), texts.astype(F32), scalars])
    grad_images, grad_texts, sums = pl.pallas_call(
        kernel,
        out_shape=(wide, wide, jax.ShapeDtypeStruct((8, 128), F32)),
        in_specs=[vmem],
        out_specs=(vmem, vmem, vmem),
        scratch_shapes=[pltpu.VMEM(shape, kind) for shape, kind in scratch] + [dma((128,)), dma((128,))],
        compiler_params=pltpu.CompilerParams(collective_id=0, has_side_effects=True, vmem_limit_bytes=VMEM_LIMIT),
        name="sigmoid_loss",
    )(given)
    return pl.pallas_call(
        finish,
        out_shape=(scalar, wide, wide, scalar, scalar),
        in_specs=[vmem] * 3,
        out_specs=(anywhere,) * 5,
        scratch_shapes=[pltpu.SMEM((1,), F32)] * 3 + [dma((5,))],
        compiler_params=pltpu.CompilerParams(vmem_limit_bytes=2**20),
        name="write_out",
    )(grad_images, grad_texts, sums)


def solution(mesh):
    in_specs = (P(("img", "txt"), None), P(("txt", "img"), None), P(), P())
    out_specs = (P(), P(("img", "txt"), None), P(("txt", "img"), None), P(), P())
    return jax.shard_map(body, mesh=mesh, in_specs=in_specs, out_specs=out_specs, check_vma=False)
```

```python
import jax
import jax.numpy as jnp
from jax import lax
from jax.experimental import pallas as pl
from jax.experimental.pallas import tpu as pltpu
from jax.sharding import PartitionSpec as P

MESH = pl.DeviceIdType.MESH
F32, BF16 = jnp.float32, jnp.bfloat16
NX, NY, NZ = 8, 8, 4
ROWS = 16
VMEM_LIMIT = 48 * 2**20
FAR_FIRST = (4, 3, 5, 2, 6, 1, 7)
NEAR_FIRST = (1, 7, 2, 6, 3, 5, 4)
LAST_Z = {4: (1, 3, 2), 3: (1, 3), 5: (1, 3)}
LAST_Y = {1: (1, 3), 7: (1, 3), 3: (2, 1), 5: (2, 1), 2: (1, 3), 6: (1, 3)}
FAR = (3, 4, 5)
NEAR = (2, 6, 1, 7)


def normalize(embed):
    wide = embed.astype(F32)
    inverse = lax.rsqrt(jnp.sum(wide * wide, axis=-1, keepdims=True) + 1e-06)
    return wide * inverse, inverse


def unnormalize(normed, inverse, grad_normed):
    inner = jnp.sum(normed * grad_normed, axis=-1, keepdims=True)
    return inverse * (grad_normed - normed * inner)


def kernel(
    given_ref,
    grad_images_ref, grad_texts_ref, sums_ref,
    XB, YB, GT, DYF, DYB, RY, RZ1, RY1, RZ, DYO, DXS, RXS, DX0, DXB, RX, RXL, RXZ, PA, PB, PC,
    ss, rs,
):
    img, txt = lax.axis_index("img"), lax.axis_index("txt")
    y, zh, c = img // (NZ * 2), (img // 2) % NZ, img % 2
    x, zl = txt // 2, txt % 2
    width = given_ref.shape[1]
    images_ref, texts_ref = given_ref.at[0:ROWS], given_ref.at[ROWS : 2 * ROWS]

    def device(dx=0, dy=0, dz=0, dl=0, dc=0):
        i = ((((y + dy) % NY) * NZ + (zh + dz) % NZ) * 2) + (c + dc) % 2
        t = ((x + dx) % NX) * 2 + (zl + dl) % 2
        return (i, t)

    sent = {}

    def send(name, src, dst, **to):
        q = len(sent)
        sent[name] = pltpu.make_async_remote_copy(
            src_ref=src, dst_ref=dst, send_sem=ss.at[q], recv_sem=rs.at[q],
            device_id=device(**to), device_id_type=MESH,
        )
        sent[name].start()

    def wait(name):
        sent[name].wait_recv()

    drained = set()

    def drain(*kinds):
        for name, copy in sent.items():
            if name not in drained and name.startswith(kinds):
                drained.add(name)
                copy.wait_send()

    others = [dict(dz=m, dl=a, dc=b) for m in range(NZ) for a in (0, 1) for b in (0, 1) if (m, a, b) != (0, 0, 0)]
    peers = [dict(dx=j) for j in range(1, NX)] + [dict(dy=j) for j in range(1, NY)] + others
    barrier = pltpu.get_barrier_semaphore()
    for peer in peers:
        pl.semaphore_signal(barrier, inc=1, device_id=device(**peer), device_id_type=MESH)

    x_norm, inv_x = normalize(images_ref[...])
    y_norm, inv_y = normalize(texts_ref[...])
    XB[0, 0, 0] = x_norm.astype(BF16)
    YB[0, 0] = y_norm.astype(BF16)
    pl.semaphore_wait(barrier, len(peers))

    for m in (1, 3, 2):
        send(f"tz{NZ - m}", YB.at[0, 0], YB.at[0, NZ - m], dz=m)
    send("xl", XB.at[0, 0, 0], XB.at[0, 0, 1], dl=1)
    for j in (6, 2, 4):
        send(f"ty{NY - j}", YB.at[0, 0], YB.at[NY - j, 0], dy=j)
    for j in (4, 3, 5):
        send(f"xo{NX - j}", XB.at[0, 0, 0], XB.at[0, NX - j, 0], dx=j)
    for j in (1, 7):
        send(f"ty{NY - j}", YB.at[0, 0], YB.at[NY - j, 0], dy=j)
    for j in (2, 6, 1, 7):
        send(f"xo{NX - j}", XB.at[0, 0, 0], XB.at[0, NX - j, 0], dx=j)
    wait("xl")
    for k in (2, 6, 1, 7):
        send(f"xp{k}", XB.at[0, 0, 1], XB.at[0, k, 1], dx=NX - k)
    for k, near, to in ((3, 2, NY - 1), (5, 6, 1)):
        wait(f"ty{near}")
        send(f"ty{k}", YB.at[near, 0], YB.at[k, 0], dy=to)
    for r in (1, 3, 2):
        wait(f"tz{r}")
        for k in (1, 7, 3, 5) if r == 2 else (1, 7):
            send(f"tp{k}{r}", YB.at[0, r], YB.at[k, r], dy=NY - k)
    send("xs0", XB.at[0, 0], XB.at[1, 0], dc=1)
    for k in (4, 3, 5):
        wait(f"xo{k}")
        send(f"xq{k}", XB.at[0, k, 0], XB.at[0, k, 1], dl=1)
    for k, rows in LAST_Z.items():
        wait(f"ty{k}")
        for r in rows:
            send(f"tw{k}{r}", YB.at[k, 0], YB.at[k, r], dz=NZ - r)
    for k, near, to in ((2, 1, NY - 1), (6, 7, 1)):
        for r in (1, 3, 2):
            wait(f"tp{near}{r}")
            send(f"tp{k}{r}", YB.at[near, r], YB.at[k, r], dy=to)
    for k in (1, 2):
        wait(f"xo{k}")
        wait(f"xp{k}")
    send("xs1", XB.at[0, pl.ds(1, 2)], XB.at[1, pl.ds(1, 2)], dc=1)
    for k in (6, 7):
        wait(f"xo{k}")
        wait(f"xp{k}")
    send("xs6", XB.at[0, pl.ds(6, 2)], XB.at[1, pl.ds(6, 2)], dc=1)
    for k in FAR:
        wait(f"xq{k}")
    send("xs3", XB.at[0, pl.ds(3, 3)], XB.at[1, pl.ds(3, 3)], dc=1)
    for k in (1, 7):
        wait(f"ty{k}")
    for k in (0, 1, 6, 3):
        wait(f"xs{k}")

    temp_row = jnp.exp(given_ref[2 * ROWS : 2 * ROWS + 1, 0:512])
    shift_row = given_ref[2 * ROWS + 1 : 2 * ROWS + 2, 0:512]
    col = lax.broadcasted_iota(jnp.int32, (1, 512), 1)
    col_core = (c + (col >> 8)) & 1
    col_x = (x + ((col >> 5) & 7)) & 7
    col_zl = (zl + ((col >> 4) & 1)) & 1
    col_id = ((y * NZ + zh) * 2 + col_core) * 256 + (col_x * 2 + col_zl) * ROWS + (col & 15)
    row = lax.broadcasted_iota(jnp.int32, (128, 1), 0)
    parts = [jnp.zeros((1, 512), F32) for _ in range(3)]

    def text_product(first):
        cols_x = XB[...].reshape(512, width)
        dy = jnp.dot(GT[pl.ds(first * 64, 128)], cols_x, preferred_element_type=F32).reshape(2, NZ, ROWS, width)
        DYF[pl.ds(first, 2)] = dy
        DYB[pl.ds(first, 2)] = dy.astype(BF16)

    def send_dy(first):
        for k in (first, first + 1):
            for r in LAST_Z.get(k, ()):
                send(f"dz{k}{r}", DYB.at[k, r], RZ1.at[k, r], dz=r)
        for k in (first, first + 1):
            if k in LAST_Y:
                r, n = LAST_Y[k]
                send(f"dy{k}", DYB.at[k, pl.ds(r, n)], RY.at[k, pl.ds(r, n)], dy=k)

    for first in (0, 4, 2, 6):
        for k in (first, first + 1):
            for r in {2: (1, 3, 2), 6: (1, 3, 2), 3: (2,), 5: (2,)}.get(k, ()):
                wait(f"tp{k}{r}")
            for r in LAST_Z.get(k, ()):
                wait(f"tw{k}{r}")
        row_y = (y + first + (row >> 6)) & 7
        row_zh = (zh + ((row >> 4) & 3)) & 3
        row_id = (x * 2 + zl) * 1024 + ((row_y * NZ + row_zh) * 2 + c) * ROWS + (row & 15)
        rows_y = YB[pl.ds(first, 2)].reshape(128, width)
        cols_x = XB[...].reshape(512, width)
        dots = lax.dot_general(rows_y, cols_x, (((1,), (1,)), ((), ())), preferred_element_type=F32)
        logits = temp_row * dots + shift_row
        match = row_id == col_id
        signed = jnp.where(match, -logits, logits)
        decay = jnp.exp(-jnp.abs(signed))
        loss = jnp.maximum(signed, 0.0) + jnp.log1p(decay)
        sig = jnp.where(signed >= 0, 1.0, decay) / (1.0 + decay)
        grad = jnp.where(match, -sig, sig)
        for n, value in enumerate((loss, grad * dots, grad)):
            parts[n] = parts[n] + jnp.sum(value, axis=0, keepdims=True)
        GT[pl.ds(first * 64, 128)] = grad.astype(BF16)
        if first != 6:
            text_product(first)
            send_dy(first)

    folded = [part[:, 0:128] + part[:, 128:256] + part[:, 256:384] + part[:, 384:512] for part in parts]
    PA[0] = jnp.concatenate(folded + [jnp.zeros((5, 128), F32)], axis=0)

    texts_all = YB[...].reshape(512, width)
    over_texts = (((0,), (0,)), ((), ()))
    groups = ((3, 3), (1, 2), (6, 2), (0, 1))
    DXS[...] = lax.dot_general(GT[:, 256:512], texts_all, over_texts, preferred_element_type=F32).reshape(NX, 2, ROWS, width)
    for first, n in groups:
        send(f"sx{first}", DXS.at[pl.ds(first, n)], RXS.at[pl.ds(first, n)], dc=1)
    text_product(6)
    send_dy(6)
    for j in FAR_FIRST:
        send(f"pa{NX - j}", PA.at[0], PA.at[NX - j], dx=j)
    DX0[...] = lax.dot_general(GT[:, 0:256], texts_all, over_texts, preferred_element_type=F32).reshape(NX, 2, ROWS, width)
    for first, n in groups:
        wait(f"sx{first}")
        both = DX0[pl.ds(first, n)] + RXS[pl.ds(first, n)]
        DX0[pl.ds(first, n)] = both
        DXB[pl.ds(first, n)] = both.astype(BF16)
        if first == 3:
            send("dl", DXB.at[pl.ds(3, 3), 1], RXL, dl=1)
        elif first:
            for k in (first, first + 1):
                send(f"dp{k}", DXB.at[k, 1], RX.at[k, 1], dx=k)
    for k in NEAR:
        send(f"dx{k}", DXB.at[k, 0], RX.at[k, 0], dx=k)

    def wide(ref):
        return ref.astype(F32)

    drain("t", "xl", "xo", "xp", "xq", "xs")

    for n, (k, rows) in enumerate(LAST_Z.items()):
        part = DYF[k, 0]
        for r in rows:
            wait(f"dz{k}{r}")
            part = part + wide(RZ1[k, r])
        DYB[k, 0] = part.astype(BF16)
        send(f"ey{k}", DYB.at[k, 0], RY1.at[n], dy=k)

    for k in range(1, NX):
        wait(f"pa{k}")
    total = PA[(0 - x) % NX]
    for a in range(1, NX):
        total = total + PA[(a - x) % NX]
    PB[0] = total
    for to in others:
        m, a, b = to["dz"], to["dl"], to["dc"]
        slot = ((NZ - m) % NZ) * 4 + a * 2 + b
        send(f"pb{slot}", PB.at[0], PB.at[slot], **to)

    for k in NEAR:
        send(f"do{k}", DYB.at[k, 0], RY.at[k, 0], dy=k)

    wait("dl")
    for n, k in enumerate(FAR):
        DXB[k, 0] = (DX0[k, 0] + wide(RXL[n])).astype(BF16)
        send(f"ex{k}", DXB.at[k, 0], RX.at[k, 0], dx=k)

    for k in LAST_Y:
        wait(f"dy{k}")
    for r in (2, 1, 3):
        part = DYF[0, r]
        for k, (low, n) in LAST_Y.items():
            if low <= r < low + n:
                part = part + wide(RY[k, r])
        DYB[0, r] = part.astype(BF16)
        send(f"ez{r}", DYB.at[0, r], RZ.at[r - 1], dz=r)

    drain("dz", "dy", "sx", "pa")

    part = DX0[0, 1]
    for k in NEAR:
        wait(f"dp{k}")
        part = part + wide(RX[k, 1])
    DXB[0, 1] = part.astype(BF16)
    send("el", DXB.at[0, 1], RXZ, dl=1)

    for slot in range(1, 16):
        wait(f"pb{slot}")
    total = None
    for m in range(NZ):
        for a in (0, 1):
            for b in (0, 1):
                term = PB[((m - zh) % NZ) * 4 + ((a - zl) % 2) * 2 + (b - c) % 2]
                total = term if total is None else total + term
    PC[0] = total
    for j in FAR_FIRST:
        send(f"pc{NY - j}", PC.at[0], PC.at[NY - j], dy=j)

    part = DYF[0, 0]
    for k in NEAR:
        wait(f"do{k}")
        part = part + wide(RY[k, 0])
    DYO[...] = part
    part = DX0[0, 0]
    for k in NEAR:
        wait(f"dx{k}")
        part = part + wide(RX[k, 0])
    DX0[0, 0] = part

    drain("pb", "dp", "dx", "dl", "do", "ey", "ex")
    scale = jnp.exp(given_ref[2 * ROWS : 2 * ROWS + 1])
    y_norm, inv_y = normalize(texts_ref[...])
    part = DYO[...]
    for r in (1, 3, 2):
        wait(f"ez{r}")
        part = part + wide(RZ[r - 1])
    for n, k in enumerate(LAST_Z):
        wait(f"ey{k}")
        part = part + wide(RY1[n])
    grad_texts_ref[...] = unnormalize(y_norm, inv_y, scale * part)

    x_norm, inv_x = normalize(images_ref[...])
    wait("el")
    part = DX0[0, 0] + wide(RXZ[...])
    for k in FAR:
        wait(f"ex{k}")
        part = part + wide(RX[k, 0])
    grad_images_ref[...] = unnormalize(x_norm, inv_x, scale * part)

    for k in range(1, NY):
        wait(f"pc{k}")
    total = PC[(0 - y) % NY]
    for a in range(1, NY):
        total = total + PC[(a - y) % NY]
    batch = float(ROWS * NX * NY * NZ * 4)
    temp = jnp.exp(given_ref[2 * ROWS : 2 * ROWS + 1, 0:128])
    sums_ref[...] = jnp.concatenate([total[0:1], temp * total[1:2], total[2:8]], axis=0) / batch

    drain("")


def finish(
    grad_images_ref, grad_texts_ref, sums_ref,
    loss_out, grad_images_out, grad_texts_out, grad_temp_out, grad_bias_out,
    loss_ref, grad_temp_ref, grad_bias_ref, sems,
):
    copies = [
        pltpu.make_async_copy(src, dst, sems.at[n])
        for n, (src, dst) in enumerate(
            (
                (grad_images_ref, grad_images_out), (grad_texts_ref, grad_texts_out),
                (loss_ref, loss_out), (grad_temp_ref, grad_temp_out), (grad_bias_ref, grad_bias_out),
            )
        )
    ]
    for copy in copies[:2]:
        copy.start()
    loss_ref[0] = jnp.sum(sums_ref[0:1])
    grad_temp_ref[0] = jnp.sum(sums_ref[1:2])
    grad_bias_ref[0] = jnp.sum(sums_ref[2:3])
    for copy in copies[2:]:
        copy.start()
    for copy in copies:
        copy.wait()


def body(images, texts, log_temp, bias):
    rows, width = images.shape
    anywhere = pl.BlockSpec(memory_space=pl.ANY)
    scalar = jax.ShapeDtypeStruct((1,), F32)
    vmem = pl.BlockSpec(memory_space=pltpu.VMEM)
    wide = jax.ShapeDtypeStruct((rows, width), F32)
    piece = (rows, width)
    scratch = [
        ((2, NX, 2) + piece, BF16),
        ((NY, NZ) + piece, BF16),
        ((512, 512), BF16),
        ((NY, NZ) + piece, F32),
        ((NY, NZ) + piece, BF16),
        ((NY, NZ) + piece, BF16),
        ((6, NZ) + piece, BF16),
        ((3,) + piece, BF16),
        ((3,) + piece, BF16),
        (piece, F32),
        ((NX, 2) + piece, F32),
        ((NX, 2) + piece, F32),
        ((NX, 2) + piece, F32),
        ((NX, 2) + piece, BF16),
        ((NX, 2) + piece, BF16),
        ((3,) + piece, BF16),
        (piece, BF16),
        ((NX, 8, 128), F32),
        ((16, 8, 128), F32),
        ((NY, 8, 128), F32),
    ]
    dma = pltpu.SemaphoreType.DMA
    scalars = jnp.concatenate([jnp.broadcast_to(v[0], (1, width)) for v in (log_temp, bias)] + [jnp.zeros((6, width), F32)])
    given = jnp.concatenate([images.astype(F32), texts.astype(F32), scalars])
    grad_images, grad_texts, sums = pl.pallas_call(
        kernel,
        out_shape=(wide, wide, jax.ShapeDtypeStruct((8, 128), F32)),
        in_specs=[vmem],
        out_specs=(vmem, vmem, vmem),
        scratch_shapes=[pltpu.VMEM(shape, kind) for shape, kind in scratch] + [dma((128,)), dma((128,))],
        compiler_params=pltpu.CompilerParams(collective_id=0, has_side_effects=True, vmem_limit_bytes=VMEM_LIMIT),
        name="sigmoid_loss",
    )(given)
    return pl.pallas_call(
        finish,
        out_shape=(scalar, wide, wide, scalar, scalar),
        in_specs=[vmem] * 3,
        out_specs=(anywhere,) * 5,
        scratch_shapes=[pltpu.SMEM((1,), F32)] * 3 + [dma((5,))],
        compiler_params=pltpu.CompilerParams(vmem_limit_bytes=2**20),
        name="write_out",
    )(grad_images, grad_texts, sums)


def solution(mesh):
    in_specs = (P(("img", "txt"), None), P(("txt", "img"), None), P(), P())
    out_specs = (P(), P(("img", "txt"), None), P(("txt", "img"), None), P(), P())
    return jax.shard_map(body, mesh=mesh, in_specs=in_specs, out_specs=out_specs, check_vma=False)
```

```python
import jax
import jax.numpy as jnp
from jax import lax
from jax.experimental import pallas as pl
from jax.experimental.pallas import tpu as pltpu
from jax.sharding import PartitionSpec as P

MESH = pl.DeviceIdType.MESH
F32, BF16 = jnp.float32, jnp.bfloat16
NX, NY, NZ = 8, 8, 4
ROWS = 16
VMEM_LIMIT = 48 * 2**20
FAR_FIRST = (4, 3, 5, 2, 6, 1, 7)
NEAR_FIRST = (1, 7, 2, 6, 3, 5, 4)
LAST_Z = {4: (1, 3, 2), 3: (1, 3), 5: (1, 3)}
LAST_Y = {1: (1, 3), 7: (1, 3), 3: (2, 1), 5: (2, 1), 2: (1, 3), 6: (1, 3)}
FAR = (3, 4, 5)
NEAR = (2, 6, 1, 7)


def normalize(embed):
    wide = embed.astype(F32)
    inverse = lax.rsqrt(jnp.sum(wide * wide, axis=-1, keepdims=True) + 1e-06)
    return wide * inverse, inverse


def unnormalize(normed, inverse, grad_normed):
    inner = jnp.sum(normed * grad_normed, axis=-1, keepdims=True)
    return inverse * (grad_normed - normed * inner)


def kernel(
    given_ref,
    grad_images_ref, grad_texts_ref, sums_ref,
    XB, YB, GT, DYF, DYB, RY, RZ1, RY1, RZ, DYO, DXS, RXS, DX0, DXB, RX, RXL, RXZ, PA, PB, PC,
    ss, rs,
):
    img, txt = lax.axis_index("img"), lax.axis_index("txt")
    y, zh, c = img // (NZ * 2), (img // 2) % NZ, img % 2
    x, zl = txt // 2, txt % 2
    width = given_ref.shape[1]
    images_ref, texts_ref = given_ref.at[0:ROWS], given_ref.at[ROWS : 2 * ROWS]

    def device(dx=0, dy=0, dz=0, dl=0, dc=0):
        i = ((((y + dy) % NY) * NZ + (zh + dz) % NZ) * 2) + (c + dc) % 2
        t = ((x + dx) % NX) * 2 + (zl + dl) % 2
        return (i, t)

    sent = {}

    def send(name, src, dst, **to):
        q = len(sent)
        sent[name] = pltpu.make_async_remote_copy(
            src_ref=src, dst_ref=dst, send_sem=ss.at[q], recv_sem=rs.at[q],
            device_id=device(**to), device_id_type=MESH,
        )
        sent[name].start()

    def wait(name):
        sent[name].wait_recv()

    drained = set()

    def drain(*kinds):
        for name, copy in sent.items():
            if name not in drained and name.startswith(kinds):
                drained.add(name)
                copy.wait_send()

    others = [dict(dz=m, dl=a, dc=b) for m in range(NZ) for a in (0, 1) for b in (0, 1) if (m, a, b) != (0, 0, 0)]
    peers = [dict(dx=j) for j in range(1, NX)] + [dict(dy=j) for j in range(1, NY)] + others
    barrier = pltpu.get_barrier_semaphore()
    for peer in peers:
        pl.semaphore_signal(barrier, inc=1, device_id=device(**peer), device_id_type=MESH)

    x_norm, inv_x = normalize(images_ref[...])
    y_norm, inv_y = normalize(texts_ref[...])
    XB[0, 0, 0] = x_norm.astype(BF16)
    YB[0, 0] = y_norm.astype(BF16)
    pl.semaphore_wait(barrier, len(peers))

    for m in (1, 3, 2):
        send(f"tz{NZ - m}", YB.at[0, 0], YB.at[0, NZ - m], dz=m)
    send("xl", XB.at[0, 0, 0], XB.at[0, 0, 1], dl=1)
    for j in (6, 2, 4):
        send(f"ty{NY - j}", YB.at[0, 0], YB.at[NY - j, 0], dy=j)
    for j in (4, 3, 5):
        send(f"xo{NX - j}", XB.at[0, 0, 0], XB.at[0, NX - j, 0], dx=j)
    for j in (1, 7):
        send(f"ty{NY - j}", YB.at[0, 0], YB.at[NY - j, 0], dy=j)
    for j in (2, 6, 1, 7):
        send(f"xo{NX - j}", XB.at[0, 0, 0], XB.at[0, NX - j, 0], dx=j)
    wait("xl")
    for k in (2, 6, 1, 7):
        send(f"xp{k}", XB.at[0, 0, 1], XB.at[0, k, 1], dx=NX - k)
    for k, near, to in ((3, 2, NY - 1), (5, 6, 1)):
        wait(f"ty{near}")
        send(f"ty{k}", YB.at[near, 0], YB.at[k, 0], dy=to)
    for r in (1, 3, 2):
        wait(f"tz{r}")
        for k in (1, 7, 3, 5) if r == 2 else (1, 7):
            send(f"tp{k}{r}", YB.at[0, r], YB.at[k, r], dy=NY - k)
    send("xs0", XB.at[0, 0], XB.at[1, 0], dc=1)
    for k in (4, 3, 5):
        wait(f"xo{k}")
        send(f"xq{k}", XB.at[0, k, 0], XB.at[0, k, 1], dl=1)
    for k, rows in LAST_Z.items():
        wait(f"ty{k}")
        for r in rows:
            send(f"tw{k}{r}", YB.at[k, 0], YB.at[k, r], dz=NZ - r)
    for k, near, to in ((2, 1, NY - 1), (6, 7, 1)):
        for r in (1, 3, 2):
            wait(f"tp{near}{r}")
            send(f"tp{k}{r}", YB.at[near, r], YB.at[k, r], dy=to)
    for k in (1, 2):
        wait(f"xo{k}")
        wait(f"xp{k}")
    send("xs1", XB.at[0, pl.ds(1, 2)], XB.at[1, pl.ds(1, 2)], dc=1)
    for k in (6, 7):
        wait(f"xo{k}")
        wait(f"xp{k}")
    send("xs6", XB.at[0, pl.ds(6, 2)], XB.at[1, pl.ds(6, 2)], dc=1)
    for k in FAR:
        wait(f"xq{k}")
    send("xs3", XB.at[0, pl.ds(3, 3)], XB.at[1, pl.ds(3, 3)], dc=1)
    for k in (1, 7):
        wait(f"ty{k}")
    for k in (0, 1, 6, 3):
        wait(f"xs{k}")

    temp_row = jnp.exp(given_ref[2 * ROWS : 2 * ROWS + 1, 0:512])
    shift_row = given_ref[2 * ROWS + 1 : 2 * ROWS + 2, 0:512]
    col = lax.broadcasted_iota(jnp.int32, (1, 512), 1)
    col_core = (c + (col >> 8)) & 1
    col_x = (x + ((col >> 5) & 7)) & 7
    col_zl = (zl + ((col >> 4) & 1)) & 1
    col_id = ((y * NZ + zh) * 2 + col_core) * 256 + (col_x * 2 + col_zl) * ROWS + (col & 15)
    row = lax.broadcasted_iota(jnp.int32, (128, 1), 0)
    parts = [jnp.zeros((1, 512), F32) for _ in range(3)]

    def text_product(first):
        cols_x = XB[...].reshape(512, width)
        dy = jnp.dot(GT[pl.ds(first * 64, 128)], cols_x, preferred_element_type=F32).reshape(2, NZ, ROWS, width)
        DYF[pl.ds(first, 2)] = dy
        DYB[pl.ds(first, 2)] = dy.astype(BF16)

    def send_dy(first):
        for k in (first, first + 1):
            for r in LAST_Z.get(k, ()):
                send(f"dz{k}{r}", DYB.at[k, r], RZ1.at[k, r], dz=r)
        for k in (first, first + 1):
            if k in LAST_Y:
                r, n = LAST_Y[k]
                send(f"dy{k}", DYB.at[k, pl.ds(r, n)], RY.at[k, pl.ds(r, n)], dy=k)

    for first in (0, 4, 2, 6):
        for k in (first, first + 1):
            for r in {2: (1, 3, 2), 6: (1, 3, 2), 3: (2,), 5: (2,)}.get(k, ()):
                wait(f"tp{k}{r}")
            for r in LAST_Z.get(k, ()):
                wait(f"tw{k}{r}")
        row_y = (y + first + (row >> 6)) & 7
        row_zh = (zh + ((row >> 4) & 3)) & 3
        row_id = (x * 2 + zl) * 1024 + ((row_y * NZ + row_zh) * 2 + c) * ROWS + (row & 15)
        rows_y = YB[pl.ds(first, 2)].reshape(128, width)
        cols_x = XB[...].reshape(512, width)
        dots = lax.dot_general(rows_y, cols_x, (((1,), (1,)), ((), ())), preferred_element_type=F32)
        logits = temp_row * dots + shift_row
        match = row_id == col_id
        signed = jnp.where(match, -logits, logits)
        decay = jnp.exp(-jnp.abs(signed))
        loss = jnp.maximum(signed, 0.0) + jnp.log1p(decay)
        sig = jnp.where(signed >= 0, 1.0, decay) / (1.0 + decay)
        grad = jnp.where(match, -sig, sig)
        for n, value in enumerate((loss, grad * dots, grad)):
            parts[n] = parts[n] + jnp.sum(value, axis=0, keepdims=True)
        GT[pl.ds(first * 64, 128)] = grad.astype(BF16)
        if first != 6:
            text_product(first)
            send_dy(first)

    folded = [part[:, 0:128] + part[:, 128:256] + part[:, 256:384] + part[:, 384:512] for part in parts]
    PA[0] = jnp.concatenate(folded + [jnp.zeros((5, 128), F32)], axis=0)

    text_product(6)
    send_dy(6)
    texts_all = YB[...].reshape(512, width)
    over_texts = (((0,), (0,)), ((), ()))
    groups = ((3, 3), (1, 2), (6, 2), (0, 1))
    DXS[...] = lax.dot_general(GT[:, 256:512], texts_all, over_texts, preferred_element_type=F32).reshape(NX, 2, ROWS, width)
    for first, n in groups:
        send(f"sx{first}", DXS.at[pl.ds(first, n)], RXS.at[pl.ds(first, n)], dc=1)
    for j in FAR_FIRST:
        send(f"pa{NX - j}", PA.at[0], PA.at[NX - j], dx=j)
    DX0[...] = lax.dot_general(GT[:, 0:256], texts_all, over_texts, preferred_element_type=F32).reshape(NX, 2, ROWS, width)
    for first, n in groups:
        wait(f"sx{first}")
        both = DX0[pl.ds(first, n)] + RXS[pl.ds(first, n)]
        DX0[pl.ds(first, n)] = both
        DXB[pl.ds(first, n)] = both.astype(BF16)
        if first == 3:
            send("dl", DXB.at[pl.ds(3, 3), 1], RXL, dl=1)
        elif first:
            for k in (first, first + 1):
                send(f"dp{k}", DXB.at[k, 1], RX.at[k, 1], dx=k)
    for k in NEAR:
        send(f"dx{k}", DXB.at[k, 0], RX.at[k, 0], dx=k)

    def wide(ref):
        return ref.astype(F32)

    drain("t", "xl", "xo", "xp", "xq", "xs")

    for n, (k, rows) in enumerate(LAST_Z.items()):
        part = DYF[k, 0]
        for r in rows:
            wait(f"dz{k}{r}")
            part = part + wide(RZ1[k, r])
        DYB[k, 0] = part.astype(BF16)
        send(f"ey{k}", DYB.at[k, 0], RY1.at[n], dy=k)

    for k in range(1, NX):
        wait(f"pa{k}")
    total = PA[(0 - x) % NX]
    for a in range(1, NX):
        total = total + PA[(a - x) % NX]
    PB[0] = total
    for to in others:
        m, a, b = to["dz"], to["dl"], to["dc"]
        slot = ((NZ - m) % NZ) * 4 + a * 2 + b
        send(f"pb{slot}", PB.at[0], PB.at[slot], **to)

    for k in NEAR:
        send(f"do{k}", DYB.at[k, 0], RY.at[k, 0], dy=k)

    wait("dl")
    for n, k in enumerate(FAR):
        DXB[k, 0] = (DX0[k, 0] + wide(RXL[n])).astype(BF16)
        send(f"ex{k}", DXB.at[k, 0], RX.at[k, 0], dx=k)

    for k in LAST_Y:
        wait(f"dy{k}")
    for r in (2, 1, 3):
        part = DYF[0, r]
        for k, (low, n) in LAST_Y.items():
            if low <= r < low + n:
                part = part + wide(RY[k, r])
        DYB[0, r] = part.astype(BF16)
        send(f"ez{r}", DYB.at[0, r], RZ.at[r - 1], dz=r)

    drain("dz", "dy", "sx", "pa")

    part = DX0[0, 1]
    for k in NEAR:
        wait(f"dp{k}")
        part = part + wide(RX[k, 1])
    DXB[0, 1] = part.astype(BF16)
    send("el", DXB.at[0, 1], RXZ, dl=1)

    for slot in range(1, 16):
        wait(f"pb{slot}")
    total = None
    for m in range(NZ):
        for a in (0, 1):
            for b in (0, 1):
                term = PB[((m - zh) % NZ) * 4 + ((a - zl) % 2) * 2 + (b - c) % 2]
                total = term if total is None else total + term
    PC[0] = total
    for j in FAR_FIRST:
        send(f"pc{NY - j}", PC.at[0], PC.at[NY - j], dy=j)

    part = DYF[0, 0]
    for k in NEAR:
        wait(f"do{k}")
        part = part + wide(RY[k, 0])
    DYO[...] = part
    part = DX0[0, 0]
    for k in NEAR:
        wait(f"dx{k}")
        part = part + wide(RX[k, 0])
    DX0[0, 0] = part

    drain("pb", "dp", "dx", "dl", "do", "ey", "ex")
    scale = jnp.exp(given_ref[2 * ROWS : 2 * ROWS + 1])
    y_norm, inv_y = normalize(texts_ref[...])
    part = DYO[...]
    for r in (1, 3, 2):
        wait(f"ez{r}")
        part = part + wide(RZ[r - 1])
    for n, k in enumerate(LAST_Z):
        wait(f"ey{k}")
        part = part + wide(RY1[n])
    grad_texts_ref[...] = unnormalize(y_norm, inv_y, scale * part)

    x_norm, inv_x = normalize(images_ref[...])
    wait("el")
    part = DX0[0, 0] + wide(RXZ[...])
    for k in FAR:
        wait(f"ex{k}")
        part = part + wide(RX[k, 0])
    grad_images_ref[...] = unnormalize(x_norm, inv_x, scale * part)

    for k in range(1, NY):
        wait(f"pc{k}")
    total = PC[(0 - y) % NY]
    for a in range(1, NY):
        total = total + PC[(a - y) % NY]
    batch = float(ROWS * NX * NY * NZ * 4)
    temp = jnp.exp(given_ref[2 * ROWS : 2 * ROWS + 1, 0:128])
    sums_ref[...] = jnp.concatenate([total[0:1], temp * total[1:2], total[2:8]], axis=0) / batch

    drain("")


def finish(
    grad_images_ref, grad_texts_ref, sums_ref,
    loss_out, grad_images_out, grad_texts_out, grad_temp_out, grad_bias_out,
    loss_ref, grad_temp_ref, grad_bias_ref, sems,
):
    copies = [
        pltpu.make_async_copy(src, dst, sems.at[n])
        for n, (src, dst) in enumerate(
            (
                (grad_images_ref, grad_images_out), (grad_texts_ref, grad_texts_out),
                (loss_ref, loss_out), (grad_temp_ref, grad_temp_out), (grad_bias_ref, grad_bias_out),
            )
        )
    ]
    for copy in copies[:2]:
        copy.start()
    loss_ref[0] = jnp.sum(sums_ref[0:1])
    grad_temp_ref[0] = jnp.sum(sums_ref[1:2])
    grad_bias_ref[0] = jnp.sum(sums_ref[2:3])
    for copy in copies[2:]:
        copy.start()
    for copy in copies:
        copy.wait()


def body(images, texts, log_temp, bias):
    rows, width = images.shape
    anywhere = pl.BlockSpec(memory_space=pl.ANY)
    scalar = jax.ShapeDtypeStruct((1,), F32)
    vmem = pl.BlockSpec(memory_space=pltpu.VMEM)
    wide = jax.ShapeDtypeStruct((rows, width), F32)
    piece = (rows, width)
    scratch = [
        ((2, NX, 2) + piece, BF16),
        ((NY, NZ) + piece, BF16),
        ((512, 512), BF16),
        ((NY, NZ) + piece, F32),
        ((NY, NZ) + piece, BF16),
        ((NY, NZ) + piece, BF16),
        ((6, NZ) + piece, BF16),
        ((3,) + piece, BF16),
        ((3,) + piece, BF16),
        (piece, F32),
        ((NX, 2) + piece, F32),
        ((NX, 2) + piece, F32),
        ((NX, 2) + piece, F32),
        ((NX, 2) + piece, BF16),
        ((NX, 2) + piece, BF16),
        ((3,) + piece, BF16),
        (piece, BF16),
        ((NX, 8, 128), F32),
        ((16, 8, 128), F32),
        ((NY, 8, 128), F32),
    ]
    dma = pltpu.SemaphoreType.DMA
    scalars = jnp.concatenate([jnp.broadcast_to(v[0], (1, width)) for v in (log_temp, bias)] + [jnp.zeros((6, width), F32)])
    given = jnp.concatenate([images.astype(F32), texts.astype(F32), scalars])
    grad_images, grad_texts, sums = pl.pallas_call(
        kernel,
        out_shape=(wide, wide, jax.ShapeDtypeStruct((8, 128), F32)),
        in_specs=[vmem],
        out_specs=(vmem, vmem, vmem),
        scratch_shapes=[pltpu.VMEM(shape, kind) for shape, kind in scratch] + [dma((128,)), dma((128,))],
        compiler_params=pltpu.CompilerParams(collective_id=0, has_side_effects=True, vmem_limit_bytes=VMEM_LIMIT),
        name="sigmoid_loss",
    )(given)
    return pl.pallas_call(
        finish,
        out_shape=(scalar, wide, wide, scalar, scalar),
        in_specs=[vmem] * 3,
        out_specs=(anywhere,) * 5,
        scratch_shapes=[pltpu.SMEM((1,), F32)] * 3 + [dma((5,))],
        compiler_params=pltpu.CompilerParams(vmem_limit_bytes=2**20),
        name="write_out",
    )(grad_images, grad_texts, sums)


def solution(mesh):
    in_specs = (P(("img", "txt"), None), P(("txt", "img"), None), P(), P())
    out_specs = (P(), P(("img", "txt"), None), P(("txt", "img"), None), P(), P())
    return jax.shard_map(body, mesh=mesh, in_specs=in_specs, out_specs=out_specs, check_vma=False)
```
